128 devices in a mesh: row: 8 (over z, core), col: 16 (over y, x).
Axes of the slice: x: 4, y: 4, z: 4, core: 2. Of those that a mesh axis runs over, the one named last changes fastest.
Arguments:
- amp_start: float32 [4096, 128, 128], P(('row', 'col')), may hold values from -6 to 6
- exch_blocks: float32 [4096, 128, 128], P(('row', 'col')), may hold values from -24 to 24
- eps_virtual: float32 [4096, 128], P(('row', 'col')), may hold values from 0.5 to 4
- pair_shift: float32 [4096], P(('row', 'col')), may hold values from -2 to -0.5
- pno_sizes: int32 [4096], P(('row', 'col')), may hold values from 120 to 128, as said below
- over_ik: bfloat16 [4096, 8, 128, 128], P(('row', 'col')), may hold values from -0.5 to 0.5
- over_kj: bfloat16 [4096, 8, 128, 128], P(('row', 'col')), may hold values from -0.5 to 0.5
- fock_ik: float32 [4096, 8], P(('row', 'col')), may hold values from -0.5 to 0.5
- fock_kj: float32 [4096, 8], P(('row', 'col')), may hold values from -0.5 to 0.5
- ik_slot: int32 [4096, 8], P(('row', 'col')), may hold values from 0 to 31
- kj_slot: int32 [4096, 8], P(('row', 'col')), may hold values from 0 to 31
- col_wants: int32 [8, 16, 32], P('row', 'col'), may hold values from 0 to 31
- row_wants: int32 [8, 16, 32], P('row', 'col'), may hold values from 0 to 31
Outputs:
- amplitudes: float32 [4096, 128, 128], P(('row', 'col'))
- residual: float32 [4096, 128, 128], P(('row', 'col'))
The draws below stay inside these ranges and needn't reach their ends.
Inputs may be any that keep to these rules, and one draw needn't show every extreme that they name: `pno_sizes`: each device holds a pair with all 128 orbitals live.
All inputs are finite; a program needn't handle non-finite values.
Results may differ from the reference program's by a relative error of at most 0.0042.
Values may be sent and summed in bfloat16 or wider, within the bound.
No kernel may reach another device: no remote copies, remote signals or barrier semaphores. Data moves between devices by JAX's collectives and lax.ppermute only.
A program may use at most 128 MiB of HBM per device.

```python
import math
import jax
import jax.numpy as jnp
from jax import lax

P_SIZE = 128
PAIRS_DEV = 32
NK = 8
CAP_C = 2
CAP_R = 4
ITERS = 2
NPAIRS = 4096
N_ROW = 8
N_COL = 16


def draw_pno_sizes(key, part):
    key = jax.random.fold_in(key, 5)
    first_key, second_key, third_key = jax.random.split(key, 3)
    smallest = P_SIZE - P_SIZE // 16
    sizes = jax.random.randint(first_key, (NPAIRS,), smallest, P_SIZE + 1)
    groups = NPAIRS // PAIRS_DEV
    spot = jax.random.randint(second_key, (groups, 1), 0, PAIRS_DEV)
    step_away = jax.random.randint(third_key, (groups, 1), 1, PAIRS_DEV)
    other_spot = (spot + step_away) % PAIRS_DEV
    local_index = jnp.arange(PAIRS_DEV)[None, :]
    full_pair = (local_index == spot).reshape(-1)
    least_pair = (local_index == other_spot).reshape(-1)
    sizes = jnp.where(least_pair, smallest, sizes)
    return jnp.where(full_pair, P_SIZE, sizes).astype(jnp.int32)


def place_ends(result, rng, low, largest):
    dims = result.shape
    index_at = [jax.random.randint(jax.random.fold_in(rng, axis), (), 0, dims[axis]) for axis in range(len(dims))]
    result = result.at[tuple(index_at)].set(low)
    longest = dims.index(max(dims))
    index_at[longest] = (index_at[longest] + 1) % dims[longest]
    return result.at[tuple(index_at)].set(largest)


def level_of(own_key, shape, cuts, least, largest):
    def one(axis_at, blocks):
        heights = jax.random.uniform(jax.random.fold_in(jax.random.fold_in(own_key, 6), axis_at), (blocks,), jnp.float32, least / len(cuts), largest / len(cuts))
        return jnp.repeat(jnp.exp(heights), shape[axis_at] // blocks).reshape((-1,) + (1,) * (len(shape) - axis_at - 1))

    factor_of = one(*cuts[0])
    for cut in cuts[1:]:
        factor_of = factor_of * one(*cut)
    return factor_of


def centred(rng, extent, scale, limit, shards=(), held_as=jnp.bfloat16):
    values = jax.random.normal(rng, extent, jnp.float32) * scale
    if len(shards) > 0:
        values = level_of(rng, extent, shards, -0.22, 0.18) * values
    return jnp.clip(values, min=-limit, max=limit).astype(held_as)


def setup_inputs(seed: int = 0) -> dict:
    splits = jax.random.split(jax.random.key(seed), 14)
    return {
        "amp_start": centred(splits[0], (NPAIRS, P_SIZE, P_SIZE), 1.0, 6.0, ((0, 128),), jnp.float32),
        "exch_blocks": centred(splits[1], (NPAIRS, P_SIZE, P_SIZE), 4.0, 24.0, ((0, 128),), jnp.float32),
        "eps_virtual": jnp.clip(jnp.exp(math.log(4.0) - 2.0794415 * jax.random.uniform(splits[2], (NPAIRS, P_SIZE), jnp.float32) ** level_of(splits[2], (NPAIRS, P_SIZE), ((0, 128),), -0.2, 0.2)), 0.5, 4.0),
        "pair_shift": jnp.clip(-2.0 + 1.5 * jax.random.uniform(splits[3], (NPAIRS,), jnp.float32) ** level_of(splits[3], (NPAIRS,), ((0, 128),), -0.2, 0.2), -2.0, -0.5),
        "pno_sizes": draw_pno_sizes(jax.random.fold_in(splits[13], 71), 0),
        "over_ik": centred(splits[5], (NPAIRS, NK, P_SIZE, P_SIZE), P_SIZE ** -0.5, 0.5, ((0, 128),)),
        "over_kj": centred(splits[6], (NPAIRS, NK, P_SIZE, P_SIZE), P_SIZE ** -0.5, 0.5, ((0, 128),)),
        "fock_ik": jnp.clip(jax.random.uniform(splits[7], (NPAIRS, NK), jnp.float32, -0.5, 0.5) * level_of(splits[7], (NPAIRS, NK), ((0, 128),), -0.4, 0.0), -0.5, 0.5),
        "fock_kj": jnp.clip(jax.random.uniform(splits[8], (NPAIRS, NK), jnp.float32, -0.5, 0.5) * level_of(splits[8], (NPAIRS, NK), ((0, 128),), -0.4, 0.0), -0.5, 0.5),
        "ik_slot": place_ends(jax.random.randint(splits[9], (NPAIRS, NK), 0, N_COL * CAP_C), jax.random.fold_in(splits[9], 1), 0, (N_COL * CAP_C) - 1).astype(jnp.int32),
        "kj_slot": place_ends(jax.random.randint(splits[10], (NPAIRS, NK), 0, N_ROW * CAP_R), jax.random.fold_in(splits[10], 1), 0, (N_ROW * CAP_R) - 1).astype(jnp.int32),
        "col_wants": place_ends(jax.random.randint(splits[11], (N_ROW, N_COL, N_COL * CAP_C), 0, PAIRS_DEV), jax.random.fold_in(splits[11], 1), 0, PAIRS_DEV - 1).astype(jnp.int32),
        "row_wants": place_ends(jax.random.randint(splits[12], (N_ROW, N_COL, N_ROW * CAP_R), 0, PAIRS_DEV), jax.random.fold_in(splits[12], 1), 0, PAIRS_DEV - 1).astype(jnp.int32),
    }


def reference(amp_start, exch_blocks, eps_virtual, pair_shift, pno_sizes, over_ik, over_kj, fock_ik, fock_kj, ik_slot, kj_slot, col_wants, row_wants):
    pno_index = jnp.arange(P_SIZE, dtype=jnp.int32)
    live_rows = (pno_index[None, :] < pno_sizes[:, None]).astype(jnp.float32)
    live_mask = live_rows[:, :, None] * live_rows[:, None, :]
    denominator = eps_virtual[:, :, None] + eps_virtual[:, None, :] - pair_shift[:, None, None]
    owner_device = jnp.arange(NPAIRS, dtype=jnp.int32) // PAIRS_DEV
    row_of = owner_device // N_COL
    col_of = owner_device % N_COL
    col_flat = col_wants.reshape(N_ROW * N_COL, N_COL * CAP_C)[owner_device]
    row_flat = row_wants.reshape(N_ROW * N_COL, N_ROW * CAP_R)[owner_device]
    ik_local = jnp.take_along_axis(col_flat, ik_slot, axis=1)
    kj_local = jnp.take_along_axis(row_flat, kj_slot, axis=1)
    ik_pair = (row_of[:, None] * N_COL + ik_slot // CAP_C) * PAIRS_DEV + ik_local
    kj_pair = ((kj_slot // CAP_R) * N_COL + col_of[:, None]) * PAIRS_DEV + kj_local
    amplitudes = live_mask * amp_start
    residual = jnp.zeros_like(amplitudes)
    for iteration in range(ITERS):
        rounded = amplitudes.astype(jnp.bfloat16)

        def one_pair(items):
            s_ik, s_kj, ik_index, kj_index, f_ik, f_kj = items
            s_ik32 = s_ik.astype(jnp.float32)
            s_kj32 = s_kj.astype(jnp.float32)
            t_ik = rounded[ik_index].astype(jnp.float32)
            t_kj = rounded[kj_index].astype(jnp.float32)
            half_ik = jnp.einsum('sab,sbc->sac', s_ik32, t_ik, precision=lax.Precision.HIGHEST)
            half_ik = lax.optimization_barrier(half_ik.astype(jnp.bfloat16)).astype(jnp.float32)
            half_kj = jnp.einsum('sab,sbc->sac', s_kj32, t_kj, precision=lax.Precision.HIGHEST)
            half_kj = lax.optimization_barrier(half_kj.astype(jnp.bfloat16)).astype(jnp.float32)
            term_ik = jnp.einsum('sac,sdc->sad', half_ik, s_ik32, precision=lax.Precision.HIGHEST)
            term_kj = jnp.einsum('sac,sdc->sad', half_kj, s_kj32, precision=lax.Precision.HIGHEST)
            return jnp.sum(f_kj[:, None, None] * term_ik + f_ik[:, None, None] * term_kj, axis=0)

        coupling = lax.map(one_pair, (over_ik, over_kj, ik_pair, kj_pair, fock_ik, fock_kj))
        residual = live_mask * (exch_blocks + denominator * amplitudes - coupling)
        amplitudes = amplitudes - residual / denominator
    return amplitudes, residual
```

```python
import functools

import jax
import jax.numpy as jnp
from jax import lax
from jax.experimental import pallas as pl
from jax.experimental.pallas import tpu as pltpu
from jax.sharding import PartitionSpec as P

F32 = jnp.float32
BF16 = jnp.bfloat16
W = 128
PAIRS = 32
NK = 8
CHUNK = 4
CHUNKS = PAIRS // CHUNK
NZ = 4
ANY = pl.BlockSpec(memory_space=pl.ANY)
SMEM = pl.BlockSpec(memory_space=pltpu.SMEM)
VMEM = pl.BlockSpec(memory_space=pltpu.VMEM)


def live(size):
    rows = lax.broadcasted_iota(jnp.int32, (W, W), 0) < size
    lanes = lax.broadcasted_iota(jnp.int32, (W, W), 1) < size
    return jnp.logical_and(rows, lanes)


def spread_body(wants, out):
    lane = lax.broadcasted_iota(jnp.int32, (1, W), 1)
    for q in range(out.shape[0]):
        out[q] = jnp.where(lane == 0, wants[0, 0, 2 * q], wants[0, 0, 2 * q + 1])


def spread_wants(col_wants):
    return pl.pallas_call(
        spread_body,
        in_specs=[SMEM],
        out_specs=VMEM,
        out_shape=jax.ShapeDtypeStruct((16, 1, W), jnp.int32),
        name="spread_wants",
    )(col_wants)


def fill_outgoing(rounded, col_asked, lists, out_col, out_row):
    me = lax.axis_index("row")
    for k in range(2 * 16):
        out_col[k] = rounded[col_asked[k // 2, 0, k % 2]]
    for dz in range(NZ):
        back = (NZ - dz) % NZ
        for part in range(2):
            for e in range(4):
                out_row[dz][4 * part + e] = rounded[lists[4 * part + back][0, 0, 4 * me + e]]


def first_body(sizes, col_asked, *refs):
    lists, amp, out_col, out_row, rounded = refs[:8], refs[8], refs[9], refs[10:14], refs[14]

    def step(p, carry):
        rounded[p] = jnp.where(live(sizes[p]), amp[p], 0.0).astype(BF16)
        return carry

    lax.fori_loop(0, PAIRS, step, 0)
    fill_outgoing(rounded, col_asked, lists, out_col, out_row)


OUTGOING = [jax.ShapeDtypeStruct((PAIRS, W, W), BF16)] + [jax.ShapeDtypeStruct((8, W, W), BF16)] * NZ


def first_outgoing(sizes, col_asked, lists, amp_start):
    return pl.pallas_call(
        first_body,
        in_specs=[SMEM, SMEM] + [SMEM] * 8 + [VMEM],
        out_specs=[VMEM] * 5,
        out_shape=OUTGOING,
        scratch_shapes=[pltpu.VMEM((PAIRS, W, W), BF16)],
        compiler_params=pltpu.CompilerParams(vmem_limit_bytes=60 * 2**20),
        name="first_outgoing",
    )(sizes, col_asked, *lists, amp_start)


def dot(a, b):
    return jnp.dot(a, b, preferred_element_type=F32)


def dot_t(a, b):
    return lax.dot_general(a, b, (((1,), (1,)), ((), ())), preferred_element_type=F32)


def two_halves(over, table, slot, fock, p, j, zero, lane):
    a, b = 2 * j, 2 * j + 1
    left = jnp.concatenate([over[p, a], over[p, b]], 1)
    blocks = jnp.concatenate(
        [
            jnp.concatenate([table[slot[a, p]], zero], 1),
            jnp.concatenate([zero, table[slot[b, p]]], 1),
        ],
        0,
    )
    return (dot(left, blocks) * jnp.where(lane < W, fock[a, p], fock[b, p])).astype(BF16)


def all_pairs(over, table, slot, fock, ready, finish):
    zero = jnp.zeros((W, W), BF16)
    lane = lax.broadcasted_iota(jnp.int32, (W, 2 * W), 1)
    halves = None
    for p in range(PAIRS + 1):
        if p < PAIRS:
            if p % CHUNK == 0:
                ready(p // CHUNK)
            following = [two_halves(over, table, slot, fock, p, j, zero, lane) for j in range(NK // 2)]
        if p > 0:
            right = jnp.concatenate([over[p - 1, s] for s in range(NK)], 1)
            finish(p - 1, dot_t(jnp.concatenate(halves, 1), right))
        halves = following


def chunk_copy(src, dst, sem, c):
    part = pl.ds(c * CHUNK, CHUNK)
    return pltpu.make_async_copy(src.at[part], dst.at[part], sem.at[c])


def row_body(first, slot, fock, sizes, shift, eps, eps_t, *refs):
    pieces, refs = refs[:8], refs[8:]
    over_h, amp_h, exch_h, refs = refs[0], refs[1], refs[2], refs[3:]
    base_h, refs = refs[0], refs[1:]
    over, table, amp, exch, base, table_sem, over_sem, amp_sem, exch_sem, base_sem = refs
    loads = []
    for dz in range(NZ):
        loads.append(pltpu.make_async_copy(pieces[dz].at[pl.ds(0, 4)], table.at[pl.ds(8 * dz, 4)], table_sem.at[dz]))
        loads.append(pltpu.make_async_copy(pieces[4 + dz].at[pl.ds(4, 4)], table.at[pl.ds(8 * dz + 4, 4)], table_sem.at[4 + dz]))
    for copy in loads:
        copy.start()
    for c in range(CHUNKS):
        chunk_copy(over_h, over, over_sem, c).start()
        chunk_copy(amp_h, amp, amp_sem, c).start()
        chunk_copy(exch_h, exch, exch_sem, c).start()
    for copy in loads:
        copy.wait()

    def ready(c):
        chunk_copy(over_h, over, over_sem, c).wait()
        chunk_copy(amp_h, amp, amp_sem, c).wait()
        chunk_copy(exch_h, exch, exch_sem, c).wait()

    def finish(p, coupling):
        here = amp[p]
        if first:
            here = jnp.where(live(sizes[p]), here, 0.0)
        denominator = eps_t[:, p : p + 1] + eps[p : p + 1, :] - shift[p]
        base[p] = exch[p] + denominator * here - coupling
        if p % CHUNK == CHUNK - 1:
            chunk_copy(base, base_h, base_sem, p // CHUNK).start()

    all_pairs(over, table, slot, fock, ready, finish)
    for c in range(CHUNKS):
        chunk_copy(base, base_h, base_sem, c).wait()


def chunked(dtype=F32):
    return pltpu.VMEM((PAIRS, W, W), dtype)


COST = pl.CostEstimate(flops=2 * 2 * 256 * W * W * W, bytes_accessed=16 * 2**20, transcendentals=0)


def row_part(first, slot, fock, sizes, shift, eps, eps_t, pieces, over, amp, exch):
    return pl.pallas_call(
        functools.partial(row_body, first),
        in_specs=[SMEM] * 4 + [VMEM] * 2 + [ANY] * 11,
        out_specs=ANY,
        out_shape=jax.ShapeDtypeStruct((PAIRS, W, W), F32),
        scratch_shapes=[
            pltpu.VMEM((PAIRS, NK, W, W), BF16),
            chunked(BF16),
            chunked(),
            chunked(),
            chunked(),
            pltpu.SemaphoreType.DMA((8,)),
        ]
        + [pltpu.SemaphoreType.DMA((CHUNKS,))] * 4,
        compiler_params=pltpu.CompilerParams(vmem_limit_bytes=60 * 2**20),
        cost_estimate=COST,
        name="row_part",
    )(slot, fock, sizes, shift, eps, eps_t, *pieces, over, amp, exch)


def col_body(first, slot, fock, sizes, shift, eps, eps_t, *refs):
    if first:
        col_asked, lists, refs = refs[0], refs[1:9], refs[9:]
    over_h, table_h, amp_h, base_h, refs = refs[0], refs[1], refs[2], refs[3], refs[4:]
    amp_out, refs = refs[0], refs[1:]
    if first:
        out_col, out_row, refs = refs[0], refs[1:5], refs[5:]
    else:
        residual_out, refs = refs[0], refs[1:]
    over, table, amp, base, third, table_sem, over_sem, amp_sem, base_sem, amp_out_sem, res_sem = refs
    load = pltpu.make_async_copy(table_h, table, table_sem)
    load.start()
    for c in range(CHUNKS):
        chunk_copy(over_h, over, over_sem, c).start()
        chunk_copy(amp_h, amp, amp_sem, c).start()
        chunk_copy(base_h, base, base_sem, c).start()
    load.wait()

    def ready(c):
        chunk_copy(over_h, over, over_sem, c).wait()
        chunk_copy(amp_h, amp, amp_sem, c).wait()
        chunk_copy(base_h, base, base_sem, c).wait()

    def finish(p, coupling):
        here = amp[p]
        alive = live(sizes[p])
        if first:
            here = jnp.where(alive, here, 0.0)
        denominator = eps_t[:, p : p + 1] + eps[p : p + 1, :] - shift[p]
        residual = jnp.where(alive, base[p] - coupling, 0.0)
        new = here - residual / denominator
        amp[p] = new
        if first:
            third[p] = new.astype(BF16)
        else:
            third[p] = residual
        if p % CHUNK == CHUNK - 1:
            chunk_copy(amp, amp_out, amp_out_sem, p // CHUNK).start()
            if not first:
                chunk_copy(third, residual_out, res_sem, p // CHUNK).start()

    all_pairs(over, table, slot, fock, ready, finish)
    if first:
        fill_outgoing(third, col_asked, lists, out_col, out_row)
    for c in range(CHUNKS):
        chunk_copy(amp, amp_out, amp_out_sem, c).wait()
        if not first:
            chunk_copy(third, residual_out, res_sem, c).wait()


def col_part(first, slot, fock, sizes, shift, eps, eps_t, asked, over, table, amp, base):
    whole = jax.ShapeDtypeStruct((PAIRS, W, W), F32)
    return pl.pallas_call(
        functools.partial(col_body, first),
        in_specs=[SMEM] * 4 + [VMEM] * 2 + [SMEM] * len(asked) + [ANY] * 4,
        out_specs=[ANY] + [VMEM] * 5 if first else [ANY] * 2,
        out_shape=[whole] + OUTGOING if first else [whole] * 2,
        scratch_shapes=[
            pltpu.VMEM((PAIRS, NK, W, W), BF16),
            chunked(BF16),
            chunked(),
            chunked(),
            chunked(BF16 if first else F32),
            pltpu.SemaphoreType.DMA,
        ]
        + [pltpu.SemaphoreType.DMA((CHUNKS,))] * 5,
        compiler_params=pltpu.CompilerParams(vmem_limit_bytes=60 * 2**20),
        cost_estimate=COST,
        name="col_part",
    )(slot, fock, sizes, shift, eps, eps_t, *asked, over, table, amp, base)


def swap_core(x):
    return lax.ppermute(x, "row", [(i, i ^ 1) for i in range(8)])


def shift_z(x, dz):
    return lax.ppermute(x, "row", [(i, (i + 2 * dz) % 8) for i in range(8)])


def row_exchange(bufs):
    same = [bufs[0]] + [shift_z(bufs[dz], dz) for dz in range(1, NZ)]
    return same + [swap_core(x) for x in same]


def shards(
    amp_start,
    exch_blocks,
    eps_virtual,
    pair_shift,
    pno_sizes,
    over_ik,
    over_kj,
    fock_ik,
    fock_kj,
    ik_slot,
    kj_slot,
    col_wants,
    row_wants,
):
    me = lax.axis_index("row")
    kj = kj_slot.T
    holder = kj // 4
    kj_place = ((me // 2 - holder // 2) % 4) * 8 + ((holder % 2) ^ (me % 2)) * 4 + kj % 4
    ik = ik_slot.T
    f_ik, f_kj = fock_ik.T, fock_kj.T
    eps_t = eps_virtual.T

    col_asked = lax.all_to_all(spread_wants(col_wants), "col", 0, 0, tiled=True)
    lists = row_exchange([row_wants, row_wants, row_wants, row_wants])
    asked = [col_asked] + lists
    amp = amp_start
    out = first_outgoing(pno_sizes, col_asked, lists, amp_start)
    for iteration in range(2):
        first = iteration == 0
        table = lax.all_to_all(out[0].reshape(16, 2, W, W), "col", 0, 0, tiled=True).reshape(PAIRS, W, W)
        pieces = row_exchange(out[1:])
        base = row_part(first, kj_place, f_ik, pno_sizes, pair_shift, eps_virtual, eps_t, pieces, over_kj, amp, exch_blocks)
        amp, *out = col_part(
            first, ik, f_kj, pno_sizes, pair_shift, eps_virtual, eps_t, asked if first else [], over_ik, table, amp, base
        )
    return (amp, out[0])


def solution(mesh):
    placed = (
        P(("row", "col"), None, None),
        P(("row", "col"), None, None),
        P(("row", "col"), None),
        P(("row", "col")),
        P(("row", "col")),
        P(("row", "col"), None, None, None),
        P(("row", "col"), None, None, None),
        P(("row", "col"), None),
        P(("row", "col"), None),
        P(("row", "col"), None),
        P(("row", "col"), None),
        P("row", "col", None),
        P("row", "col", None),
    )
    return jax.shard_map(
        shards,
        mesh=mesh,
        in_specs=placed,
        out_specs=(P(("row", "col"), None, None), P(("row", "col"), None, None)),
        check_vma=False,
    )
```

```python
import functools

import jax
import jax.numpy as jnp
from jax import lax
from jax.experimental import pallas as pl
from jax.experimental.pallas import tpu as pltpu
from jax.sharding import PartitionSpec as P

F32 = jnp.float32
BF16 = jnp.bfloat16
W = 128
PAIRS = 32
NK = 8
CUTS = (0, 4, 12, 20, 28, 32)
CHUNKS = len(CUTS) - 1
AHEAD = 2
NZ = 4
ANY = pl.BlockSpec(memory_space=pl.ANY)
SMEM = pl.BlockSpec(memory_space=pltpu.SMEM)
VMEM = pl.BlockSpec(memory_space=pltpu.VMEM)


def live(size):
    rows = lax.broadcasted_iota(jnp.int32, (W, W), 0) < size
    lanes = lax.broadcasted_iota(jnp.int32, (W, W), 1) < size
    return jnp.logical_and(rows, lanes)


def spread_body(wants, out):
    lane = lax.broadcasted_iota(jnp.int32, (1, W), 1)
    for q in range(out.shape[0]):
        out[q] = jnp.where(lane == 0, wants[0, 0, 2 * q], wants[0, 0, 2 * q + 1])


def spread_wants(col_wants):
    return pl.pallas_call(
        spread_body,
        in_specs=[SMEM],
        out_specs=VMEM,
        out_shape=jax.ShapeDtypeStruct((16, 1, W), jnp.int32),
        name="spread_wants",
    )(col_wants)


def start_outgoing(rounded, col_asked, lists, out_col, out_row, sems):
    me = lax.axis_index("row")
    copies = []
    for dz in range(NZ):
        back = (NZ - dz) % NZ
        for part in range(2):
            for e in range(4):
                wanted = lists[4 * part + back][0, 0, 4 * me + e]
                spot = 4 * part + e
                copies.append(pltpu.make_async_copy(rounded.at[wanted], out_row[dz].at[spot], sems.at[8 * dz + spot]))
    for k in range(PAIRS):
        wanted = col_asked[k // 2, 0, k % 2]
        copies.append(pltpu.make_async_copy(rounded.at[wanted], out_col.at[k], sems.at[PAIRS + k]))
    for copy in copies:
        copy.start()
    return copies


def first_body(sizes, col_asked, *refs):
    lists, amp, out_col, out_row, rounded, sems = refs[:8], refs[8], refs[9], refs[10:14], refs[14], refs[15]

    def step(p, carry):
        rounded[p] = jnp.where(live(sizes[p]), amp[p], 0.0).astype(BF16)
        return carry

    lax.fori_loop(0, PAIRS, step, 0, unroll=4)
    for copy in start_outgoing(rounded, col_asked, lists, out_col, out_row, sems):
        copy.wait()


OUTGOING = [jax.ShapeDtypeStruct((PAIRS, W, W), BF16)] + [jax.ShapeDtypeStruct((8, W, W), BF16)] * NZ


def first_outgoing(sizes, asked, amp_start):
    return pl.pallas_call(
        first_body,
        in_specs=[SMEM] + [SMEM] * 9 + [VMEM],
        out_specs=[ANY] * 5,
        out_shape=OUTGOING,
        scratch_shapes=[pltpu.VMEM((PAIRS, W, W), BF16), pltpu.SemaphoreType.DMA((2 * PAIRS,))],
        compiler_params=pltpu.CompilerParams(vmem_limit_bytes=60 * 2**20),
        name="first_outgoing",
    )(sizes, *asked, amp_start)


def dot(a, b):
    return jnp.dot(a, b, preferred_element_type=F32)


def dot_t(a, b):
    return lax.dot_general(a, b, (((1,), (1,)), ((), ())), preferred_element_type=F32)


def two_halves(over, table, slot, fock, p, j, zero, lane):
    a, b = 2 * j, 2 * j + 1
    left = jnp.concatenate([over[p, a], over[p, b]], 1)
    blocks = jnp.concatenate(
        [
            jnp.concatenate([table[slot[a, p]], zero], 1),
            jnp.concatenate([zero, table[slot[b, p]]], 1),
        ],
        0,
    )
    return (dot(left, blocks) * jnp.where(lane < W, fock[a, p], fock[b, p])).astype(BF16)


def all_pairs(over, table, slot, fock, ready, finish):
    zero = jnp.zeros((W, W), BF16)
    lane = lax.broadcasted_iota(jnp.int32, (W, 2 * W), 1)
    halves = None
    for p in range(PAIRS + 1):
        if p < PAIRS:
            if p in CUTS:
                ready(CUTS.index(p))
            following = [two_halves(over, table, slot, fock, p, j, zero, lane) for j in range(NK // 2)]
        if p > 0:
            right = jnp.concatenate([over[p - 1, s] for s in range(NK)], 1)
            finish(p - 1, dot_t(jnp.concatenate(halves, 1), right))
        halves = following


def chunk_copy(src, dst, sem, c):
    part = pl.ds(CUTS[c], CUTS[c + 1] - CUTS[c])
    return pltpu.make_async_copy(src.at[part], dst.at[part], sem.at[c])


def row_body(first, slot, fock, sizes, shift, eps, *refs):
    pieces, refs = refs[:8], refs[8:]
    over_h, amp_h, exch_h, refs = refs[0], refs[1], refs[2], refs[3:]
    base_h, refs = refs[0], refs[1:]
    over, table, amp, exch, base, table_sem, over_sem, amp_sem, exch_sem, base_sem = refs
    me = lax.axis_index("row")
    core = lax.rem(me, 2)
    loads = []
    for dz in range(NZ):
        chip = 8 * lax.rem(me // 2 + NZ - dz, NZ)
        for part, from_core in ((0, core), (1, 1 - core)):
            source = pieces[NZ * part + dz].at[pl.ds(4 * part, 4)]
            loads.append(pltpu.make_async_copy(source, table.at[pl.ds(chip + 4 * from_core, 4)], table_sem.at[NZ * part + dz]))
    for copy in loads:
        copy.start()
    def fetch(c):
        chunk_copy(over_h, over, over_sem, c).start()
        chunk_copy(amp_h, amp, amp_sem, c).start()
        chunk_copy(exch_h, exch, exch_sem, c).start()

    for c in range(AHEAD):
        fetch(c)
    eps_t = jnp.transpose(eps[...])
    for copy in loads:
        copy.wait()

    def ready(c):
        if c + AHEAD < CHUNKS:
            fetch(c + AHEAD)
        chunk_copy(over_h, over, over_sem, c).wait()
        chunk_copy(amp_h, amp, amp_sem, c).wait()
        chunk_copy(exch_h, exch, exch_sem, c).wait()

    def finish(p, coupling):
        here = amp[p]
        if first:
            here = jnp.where(live(sizes[p]), here, 0.0)
        denominator = eps_t[:, p : p + 1] + eps[p : p + 1, :] - shift[p]
        base[p] = exch[p] + denominator * here - coupling
        if p + 1 in CUTS:
            chunk_copy(base, base_h, base_sem, CUTS.index(p + 1) - 1).start()

    all_pairs(over, table, slot, fock, ready, finish)
    for c in range(CHUNKS):
        chunk_copy(base, base_h, base_sem, c).wait()


def chunked(dtype=F32):
    return pltpu.VMEM((PAIRS, W, W), dtype)


FLOPS = 2 * 2 * 256 * W * W * W


def cost(times):
    return pl.CostEstimate(flops=times * FLOPS, bytes_accessed=16 * 2**20, transcendentals=0)


def row_part(first, slot, fock, sizes, shift, eps, pieces, over, amp, exch):
    return pl.pallas_call(
        functools.partial(row_body, first),
        in_specs=[SMEM] * 4 + [VMEM] + [ANY] * 11,
        out_specs=ANY,
        out_shape=jax.ShapeDtypeStruct((PAIRS, W, W), F32),
        scratch_shapes=[
            pltpu.VMEM((PAIRS, NK, W, W), BF16),
            chunked(BF16),
            chunked(),
            chunked(),
            chunked(),
            pltpu.SemaphoreType.DMA((8,)),
        ]
        + [pltpu.SemaphoreType.DMA((CHUNKS,))] * 4,
        compiler_params=pltpu.CompilerParams(vmem_limit_bytes=60 * 2**20),
        cost_estimate=cost(12),
        name="row_part",
    )(slot, fock, sizes, shift, eps, *pieces, over, amp, exch)


def col_body(first, slot, fock, sizes, shift, eps, *refs):
    if first:
        col_asked, lists, refs = refs[0], refs[1:9], refs[9:]
    over_h, table_h, amp_h, base_h, refs = refs[0], refs[1], refs[2], refs[3], refs[4:]
    amp_out, refs = refs[0], refs[1:]
    if first:
        out_col, out_row, refs = refs[0], refs[1:5], refs[5:]
    else:
        third_out, refs = refs[0], refs[1:]
    over, table, amp, base, third, table_sem, over_sem, amp_sem, base_sem, amp_out_sem, third_sem, sems = refs
    load = pltpu.make_async_copy(table_h, table, table_sem)
    load.start()
    def fetch(c):
        chunk_copy(over_h, over, over_sem, c).start()
        chunk_copy(amp_h, amp, amp_sem, c).start()
        chunk_copy(base_h, base, base_sem, c).start()

    for c in range(AHEAD):
        fetch(c)
    eps_t = jnp.transpose(eps[...])
    load.wait()

    def ready(c):
        if c + AHEAD < CHUNKS:
            fetch(c + AHEAD)
        chunk_copy(over_h, over, over_sem, c).wait()
        chunk_copy(amp_h, amp, amp_sem, c).wait()
        chunk_copy(base_h, base, base_sem, c).wait()

    def finish(p, coupling):
        here = amp[p]
        alive = live(sizes[p])
        if first:
            here = jnp.where(alive, here, 0.0)
        denominator = eps_t[:, p : p + 1] + eps[p : p + 1, :] - shift[p]
        residual = jnp.where(alive, base[p] - coupling, 0.0)
        new = here - residual / denominator
        amp[p] = new
        if first:
            third[p] = new.astype(BF16)
        else:
            third[p] = residual
        if p + 1 in CUTS:
            chunk_copy(amp, amp_out, amp_out_sem, CUTS.index(p + 1) - 1).start()
            if not first:
                chunk_copy(third, third_out, third_sem, CUTS.index(p + 1) - 1).start()

    all_pairs(over, table, slot, fock, ready, finish)
    if first:
        for copy in start_outgoing(third, col_asked, lists, out_col, out_row, sems):
            copy.wait()
    for c in range(CHUNKS):
        chunk_copy(amp, amp_out, amp_out_sem, c).wait()
        if not first:
            chunk_copy(third, third_out, third_sem, c).wait()


def col_part(first, slot, fock, sizes, shift, eps, asked, over, table, amp, base):
    whole = jax.ShapeDtypeStruct((PAIRS, W, W), F32)
    return pl.pallas_call(
        functools.partial(col_body, first),
        in_specs=[SMEM] * 4 + [VMEM] + [SMEM] * len(asked) + [ANY] * 4,
        out_specs=[ANY] * 6 if first else [ANY] * 2,
        out_shape=[whole] + OUTGOING if first else [whole] * 2,
        scratch_shapes=[
            pltpu.VMEM((PAIRS, NK, W, W), BF16),
            chunked(BF16),
            chunked(),
            chunked(),
            chunked(BF16 if first else F32),
            pltpu.SemaphoreType.DMA,
        ]
        + [pltpu.SemaphoreType.DMA((CHUNKS,))] * 5
        + [pltpu.SemaphoreType.DMA((2 * PAIRS,))],
        compiler_params=pltpu.CompilerParams(vmem_limit_bytes=60 * 2**20),
        cost_estimate=cost(1),
        name="col_part",
    )(slot, fock, sizes, shift, eps, *asked, over, table, amp, base)


def swap_core(x):
    return lax.ppermute(x, "row", [(i, i ^ 1) for i in range(8)])


def shift_z(x, dz):
    return lax.ppermute(x, "row", [(i, (i + 2 * dz) % 8) for i in range(8)])


def row_exchange(bufs):
    same = [bufs[0]] + [shift_z(bufs[dz], dz) for dz in range(1, NZ)]
    return same + [swap_core(x) for x in same]


def shards(
    amp_start,
    exch_blocks,
    eps_virtual,
    pair_shift,
    pno_sizes,
    over_ik,
    over_kj,
    fock_ik,
    fock_kj,
    ik_slot,
    kj_slot,
    col_wants,
    row_wants,
):
    kj, ik = kj_slot.T, ik_slot.T
    f_ik, f_kj = fock_ik.T, fock_kj.T
    col_asked = lax.all_to_all(spread_wants(col_wants), "col", 0, 0, tiled=True)
    asked = [col_asked] + row_exchange([row_wants] * NZ)
    amp = amp_start
    out = first_outgoing(pno_sizes, asked, amp_start)
    for iteration in range(2):
        first = iteration == 0
        pieces = row_exchange(out[1:])
        table = lax.all_to_all(out[0].reshape(16, 2, W, W), "col", 0, 0, tiled=True).reshape(PAIRS, W, W)
        base = row_part(first, kj, f_ik, pno_sizes, pair_shift, eps_virtual, pieces, over_kj, amp, exch_blocks)
        amp, *out = col_part(
            first, ik, f_kj, pno_sizes, pair_shift, eps_virtual, asked if first else [], over_ik, table, amp, base
        )
    return (amp, out[0])


def solution(mesh):
    placed = (
        P(("row", "col"), None, None),
        P(("row", "col"), None, None),
        P(("row", "col"), None),
        P(("row", "col")),
        P(("row", "col")),
        P(("row", "col"), None, None, None),
        P(("row", "col"), None, None, None),
        P(("row", "col"), None),
        P(("row", "col"), None),
        P(("row", "col"), None),
        P(("row", "col"), None),
        P("row", "col", None),
        P("row", "col", None),
    )
    return jax.shard_map(
        shards,
        mesh=mesh,
        in_specs=placed,
        out_specs=(P(("row", "col"), None, None), P(("row", "col"), None, None)),
        check_vma=False,
    )
```

```python
import functools

import jax
import jax.numpy as jnp
from jax import lax
from jax.experimental import pallas as pl
from jax.experimental.pallas import tpu as pltpu
from jax.sharding import PartitionSpec as P

F32 = jnp.float32
BF16 = jnp.bfloat16
W = 128
PAIRS = 32
NK = 8
CUTS = (0, 4, 12, 20, 28, 32)
CHUNKS = len(CUTS) - 1
AHEAD = 2
NZ = 4
ANY = pl.BlockSpec(memory_space=pl.ANY)
SMEM = pl.BlockSpec(memory_space=pltpu.SMEM)
VMEM = pl.BlockSpec(memory_space=pltpu.VMEM)


def live(size):
    rows = lax.broadcasted_iota(jnp.int32, (W, W), 0) < size
    lanes = lax.broadcasted_iota(jnp.int32, (W, W), 1) < size
    return jnp.logical_and(rows, lanes)


def spread_body(wants, out):
    lane = lax.broadcasted_iota(jnp.int32, (1, W), 1)
    for q in range(out.shape[0]):
        out[q] = jnp.where(lane == 0, wants[0, 0, 2 * q], wants[0, 0, 2 * q + 1])


def spread_wants(col_wants):
    return pl.pallas_call(
        spread_body,
        in_specs=[SMEM],
        out_specs=VMEM,
        out_shape=jax.ShapeDtypeStruct((16, 1, W), jnp.int32),
        name="spread_wants",
    )(col_wants)


def start_outgoing(rounded, col_asked, lists, out_col, out_row, sems):
    me = lax.axis_index("row")
    copies = []
    for dz in range(NZ):
        back = (NZ - dz) % NZ
        for part in range(2):
            for e in range(4):
                wanted = lists[4 * part + back][0, 0, 4 * me + e]
                spot = 4 * part + e
                copies.append(pltpu.make_async_copy(rounded.at[wanted], out_row[dz].at[spot], sems.at[8 * dz + spot]))
    for k in range(PAIRS):
        wanted = col_asked[k // 2, 0, k % 2]
        copies.append(pltpu.make_async_copy(rounded.at[wanted], out_col.at[k], sems.at[PAIRS + k]))
    for copy in copies:
        copy.start()
    return copies


def first_body(sizes, col_asked, *refs):
    lists, amp, out_col, out_row, rounded, sems = refs[:8], refs[8], refs[9], refs[10:14], refs[14], refs[15]

    def step(p, carry):
        rounded[p] = jnp.where(live(sizes[p]), amp[p], 0.0).astype(BF16)
        return carry

    lax.fori_loop(0, PAIRS, step, 0, unroll=4)
    for copy in start_outgoing(rounded, col_asked, lists, out_col, out_row, sems):
        copy.wait()


OUTGOING = [jax.ShapeDtypeStruct((PAIRS, W, W), BF16)] + [jax.ShapeDtypeStruct((8, W, W), BF16)] * NZ


def first_outgoing(sizes, asked, amp_start):
    return pl.pallas_call(
        first_body,
        in_specs=[SMEM] + [SMEM] * 9 + [VMEM],
        out_specs=[ANY] * 5,
        out_shape=OUTGOING,
        scratch_shapes=[pltpu.VMEM((PAIRS, W, W), BF16), pltpu.SemaphoreType.DMA((2 * PAIRS,))],
        compiler_params=pltpu.CompilerParams(vmem_limit_bytes=52 * 2**20),
        name="first_outgoing",
    )(sizes, *asked, amp_start)


def dot(a, b):
    return jnp.dot(a, b, preferred_element_type=F32)


def dot_t(a, b):
    return lax.dot_general(a, b, (((1,), (1,)), ((), ())), preferred_element_type=F32)


def two_halves(over, table, slot, fock, p, j, zero, lane):
    a, b = 2 * j, 2 * j + 1
    left = jnp.concatenate([over[p, a], over[p, b]], 1)
    blocks = jnp.concatenate(
        [
            jnp.concatenate([table[slot[a, p]], zero], 1),
            jnp.concatenate([zero, table[slot[b, p]]], 1),
        ],
        0,
    )
    return (dot(left, blocks) * jnp.where(lane < W, fock[a, p], fock[b, p])).astype(BF16)


def all_pairs(over, table, slot, fock, ready, finish):
    zero = jnp.zeros((W, W), BF16)
    lane = lax.broadcasted_iota(jnp.int32, (W, 2 * W), 1)
    halves = None
    for p in range(PAIRS + 1):
        if p < PAIRS:
            if p in CUTS:
                ready(CUTS.index(p))
            following = [two_halves(over, table, slot, fock, p, j, zero, lane) for j in range(NK // 2)]
        if p > 0:
            right = jnp.concatenate([over[p - 1, s] for s in range(NK)], 1)
            finish(p - 1, dot_t(jnp.concatenate(halves, 1), right))
        halves = following


def chunk_copy(src, dst, sem, c):
    part = pl.ds(CUTS[c], CUTS[c + 1] - CUTS[c])
    return pltpu.make_async_copy(src.at[part], dst.at[part], sem.at[c])


def row_body(first, slot, fock, sizes, shift, eps, *refs):
    pieces, refs = refs[:8], refs[8:]
    over_h, amp_h, exch_h, refs = refs[0], refs[1], refs[2], refs[3:]
    base_h, refs = refs[0], refs[1:]
    over, table, amp, exch, base, table_sem, over_sem, amp_sem, exch_sem, base_sem = refs
    me = lax.axis_index("row")
    core = lax.rem(me, 2)
    loads = []
    for dz in range(NZ):
        chip = 8 * lax.rem(me // 2 + NZ - dz, NZ)
        for part, from_core in ((0, core), (1, 1 - core)):
            source = pieces[NZ * part + dz].at[pl.ds(4 * part, 4)]
            loads.append(pltpu.make_async_copy(source, table.at[pl.ds(chip + 4 * from_core, 4)], table_sem.at[NZ * part + dz]))
    for copy in loads:
        copy.start()
    def fetch(c):
        chunk_copy(over_h, over, over_sem, c).start()
        chunk_copy(amp_h, amp, amp_sem, c).start()
        chunk_copy(exch_h, exch, exch_sem, c).start()

    for c in range(AHEAD):
        fetch(c)
    eps_t = jnp.transpose(eps[...])
    for copy in loads:
        copy.wait()

    def ready(c):
        if c + AHEAD < CHUNKS:
            fetch(c + AHEAD)
        chunk_copy(over_h, over, over_sem, c).wait()
        chunk_copy(amp_h, amp, amp_sem, c).wait()
        chunk_copy(exch_h, exch, exch_sem, c).wait()

    def finish(p, coupling):
        here = amp[p]
        if first:
            here = jnp.where(live(sizes[p]), here, 0.0)
        denominator = eps_t[:, p : p + 1] + eps[p : p + 1, :] - shift[p]
        base[p] = exch[p] + denominator * here - coupling
        if p + 1 in CUTS:
            chunk_copy(base, base_h, base_sem, CUTS.index(p + 1) - 1).start()

    all_pairs(over, table, slot, fock, ready, finish)
    for c in range(CHUNKS):
        chunk_copy(base, base_h, base_sem, c).wait()


def chunked(dtype=F32):
    return pltpu.VMEM((PAIRS, W, W), dtype)


FLOPS = 2 * 2 * 256 * W * W * W


def cost(times):
    return pl.CostEstimate(flops=times * FLOPS, bytes_accessed=16 * 2**20, transcendentals=0)


def row_part(first, slot, fock, sizes, shift, eps, pieces, over, amp, exch):
    return pl.pallas_call(
        functools.partial(row_body, first),
        in_specs=[SMEM] * 4 + [VMEM] + [VMEM] * 8 + [ANY] * 3,
        out_specs=ANY,
        out_shape=jax.ShapeDtypeStruct((PAIRS, W, W), F32),
        scratch_shapes=[
            pltpu.VMEM((PAIRS, NK, W, W), BF16),
            chunked(BF16),
            chunked(),
            chunked(),
            chunked(),
            pltpu.SemaphoreType.DMA((8,)),
        ]
        + [pltpu.SemaphoreType.DMA((CHUNKS,))] * 4,
        compiler_params=pltpu.CompilerParams(vmem_limit_bytes=52 * 2**20),
        cost_estimate=cost(3),
        name="row_part",
    )(slot, fock, sizes, shift, eps, *pieces, over, amp, exch)


def col_body(first, slot, fock, sizes, shift, eps, *refs):
    if first:
        col_asked, lists, refs = refs[0], refs[1:9], refs[9:]
    over_h, table, amp_h, base_h, refs = refs[0], refs[1], refs[2], refs[3], refs[4:]
    amp_out, refs = refs[0], refs[1:]
    if first:
        out_col, out_row, refs = refs[0], refs[1:5], refs[5:]
    else:
        third_out, refs = refs[0], refs[1:]
    over, amp, base, third, over_sem, amp_sem, base_sem, amp_out_sem, third_sem, sems = refs
    def fetch(c):
        chunk_copy(over_h, over, over_sem, c).start()
        chunk_copy(amp_h, amp, amp_sem, c).start()
        chunk_copy(base_h, base, base_sem, c).start()

    for c in range(AHEAD):
        fetch(c)
    eps_t = jnp.transpose(eps[...])

    def ready(c):
        if c + AHEAD < CHUNKS:
            fetch(c + AHEAD)
        chunk_copy(over_h, over, over_sem, c).wait()
        chunk_copy(amp_h, amp, amp_sem, c).wait()
        chunk_copy(base_h, base, base_sem, c).wait()

    def finish(p, coupling):
        here = amp[p]
        alive = live(sizes[p])
        if first:
            here = jnp.where(alive, here, 0.0)
        denominator = eps_t[:, p : p + 1] + eps[p : p + 1, :] - shift[p]
        residual = jnp.where(alive, base[p] - coupling, 0.0)
        new = here - residual / denominator
        amp[p] = new
        if first:
            third[p] = new.astype(BF16)
        else:
            third[p] = residual
        if p + 1 in CUTS:
            chunk_copy(amp, amp_out, amp_out_sem, CUTS.index(p + 1) - 1).start()
            if not first:
                chunk_copy(third, third_out, third_sem, CUTS.index(p + 1) - 1).start()

    all_pairs(over, table, slot, fock, ready, finish)
    if first:
        for copy in start_outgoing(third, col_asked, lists, out_col, out_row, sems):
            copy.wait()
    for c in range(CHUNKS):
        chunk_copy(amp, amp_out, amp_out_sem, c).wait()
        if not first:
            chunk_copy(third, third_out, third_sem, c).wait()


def col_part(first, slot, fock, sizes, shift, eps, asked, over, table, amp, base):
    whole = jax.ShapeDtypeStruct((PAIRS, W, W), F32)
    return pl.pallas_call(
        functools.partial(col_body, first),
        in_specs=[SMEM] * 4 + [VMEM] + [SMEM] * len(asked) + [ANY, VMEM, ANY, ANY],
        out_specs=[ANY] * 6 if first else [ANY] * 2,
        out_shape=[whole] + OUTGOING if first else [whole] * 2,
        scratch_shapes=[
            pltpu.VMEM((PAIRS, NK, W, W), BF16),
            chunked(),
            chunked(),
            chunked(BF16 if first else F32),
        ]
        + [pltpu.SemaphoreType.DMA((CHUNKS,))] * 5
        + [pltpu.SemaphoreType.DMA((2 * PAIRS,))],
        compiler_params=pltpu.CompilerParams(vmem_limit_bytes=52 * 2**20),
        cost_estimate=cost(1),
        name="col_part",
    )(slot, fock, sizes, shift, eps, *asked, over, table, amp, base)


def swap_core(x):
    return lax.ppermute(x, "row", [(i, i ^ 1) for i in range(8)])


def shift_z(x, dz):
    return lax.ppermute(x, "row", [(i, (i + 2 * dz) % 8) for i in range(8)])


def row_exchange(bufs):
    same = [bufs[0]] + [shift_z(bufs[dz], dz) for dz in range(1, NZ)]
    return same + [swap_core(x) for x in same]


def shards(
    amp_start,
    exch_blocks,
    eps_virtual,
    pair_shift,
    pno_sizes,
    over_ik,
    over_kj,
    fock_ik,
    fock_kj,
    ik_slot,
    kj_slot,
    col_wants,
    row_wants,
):
    kj, ik = kj_slot.T, ik_slot.T
    f_ik, f_kj = fock_ik.T, fock_kj.T
    col_asked = lax.all_to_all(spread_wants(col_wants), "col", 0, 0, tiled=True)
    asked = [col_asked] + row_exchange([row_wants] * NZ)
    amp = amp_start
    out = first_outgoing(pno_sizes, asked, amp_start)
    for iteration in range(2):
        first = iteration == 0
        pieces = row_exchange(out[1:])
        table = lax.all_to_all(out[0].reshape(16, 2, W, W), "col", 0, 0, tiled=True).reshape(PAIRS, W, W)
        base = row_part(first, kj, f_ik, pno_sizes, pair_shift, eps_virtual, pieces, over_kj, amp, exch_blocks)
        amp, *out = col_part(
            first, ik, f_kj, pno_sizes, pair_shift, eps_virtual, asked if first else [], over_ik, table, amp, base
        )
    return (amp, out[0])


def solution(mesh):
    placed = (
        P(("row", "col"), None, None),
        P(("row", "col"), None, None),
        P(("row", "col"), None),
        P(("row", "col")),
        P(("row", "col")),
        P(("row", "col"), None, None, None),
        P(("row", "col"), None, None, None),
        P(("row", "col"), None),
        P(("row", "col"), None),
        P(("row", "col"), None),
        P(("row", "col"), None),
        P("row", "col", None),
        P("row", "col", None),
    )
    return jax.shard_map(
        shards,
        mesh=mesh,
        in_specs=placed,
        out_specs=(P(("row", "col"), None, None), P(("row", "col"), None, None)),
        check_vma=False,
    )
```

```python
import functools

import jax
import jax.numpy as jnp
from jax import lax
from jax.experimental import pallas as pl
from jax.experimental.pallas import tpu as pltpu
from jax.sharding import PartitionSpec as P

F32 = jnp.float32
BF16 = jnp.bfloat16
W = 128
PAIRS = 32
NK = 8
CUTS = (0, 4, 12, 20, 28, 32)
CHUNKS = len(CUTS) - 1
AHEAD = 2
NZ = 4
ANY = pl.BlockSpec(memory_space=pl.ANY)
SMEM = pl.BlockSpec(memory_space=pltpu.SMEM)
VMEM = pl.BlockSpec(memory_space=pltpu.VMEM)


def live(size):
    rows = lax.broadcasted_iota(jnp.int32, (W, W), 0) < size
    lanes = lax.broadcasted_iota(jnp.int32, (W, W), 1) < size
    return jnp.logical_and(rows, lanes)


def spread_body(wants, out):
    lane = lax.broadcasted_iota(jnp.int32, (1, W), 1)
    for q in range(out.shape[0]):
        out[q] = jnp.where(lane == 0, wants[0, 0, 2 * q], wants[0, 0, 2 * q + 1])


def spread_wants(col_wants):
    return pl.pallas_call(
        spread_body,
        in_specs=[SMEM],
        out_specs=VMEM,
        out_shape=jax.ShapeDtypeStruct((16, 1, W), jnp.int32),
        name="spread_wants",
    )(col_wants)


def start_outgoing(rounded, col_asked, lists, out_col, out_row, sems):
    copies = []
    for k in range(PAIRS):
        wanted = col_asked[k // 2, 0, k % 2]
        copies.append(pltpu.make_async_copy(rounded.at[wanted], out_col.at[k], sems.at[k]))
    for copy in copies:
        copy.start()
    me = lax.axis_index("row")
    for dz in range(NZ):
        back = (NZ - dz) % NZ
        for part in range(2):
            for e in range(4):
                out_row[dz][4 * part + e] = rounded[lists[4 * part + back][0, 0, 4 * me + e]]
    return copies


def first_body(sizes, col_asked, *refs):
    lists, amp, out_col, out_row, rounded, sems = refs[:8], refs[8], refs[9], refs[10:14], refs[14], refs[15]

    def step(p, carry):
        rounded[p] = jnp.where(live(sizes[p]), amp[p], 0.0).astype(BF16)
        return carry

    lax.fori_loop(0, PAIRS, step, 0, unroll=4)
    for copy in start_outgoing(rounded, col_asked, lists, out_col, out_row, sems):
        copy.wait()


OUTGOING = [jax.ShapeDtypeStruct((PAIRS, W, W), BF16)] + [jax.ShapeDtypeStruct((8, W, W), BF16)] * NZ


def first_outgoing(sizes, asked, amp_start):
    return pl.pallas_call(
        first_body,
        in_specs=[SMEM] + [SMEM] * 9 + [VMEM],
        out_specs=[ANY] + [VMEM] * NZ,
        out_shape=OUTGOING,
        scratch_shapes=[pltpu.VMEM((PAIRS, W, W), BF16), pltpu.SemaphoreType.DMA((PAIRS,))],
        compiler_params=pltpu.CompilerParams(vmem_limit_bytes=52 * 2**20),
        name="first_outgoing",
    )(sizes, *asked, amp_start)


def dot(a, b):
    return jnp.dot(a, b, preferred_element_type=F32)


def dot_t(a, b):
    return lax.dot_general(a, b, (((1,), (1,)), ((), ())), preferred_element_type=F32)


def two_halves(over, table, slot, fock, p, j, zero, lane):
    a, b = 2 * j, 2 * j + 1
    left = jnp.concatenate([over[p, a], over[p, b]], 1)
    blocks = jnp.concatenate(
        [
            jnp.concatenate([table[slot[a, p]], zero], 1),
            jnp.concatenate([zero, table[slot[b, p]]], 1),
        ],
        0,
    )
    return (dot(left, blocks) * jnp.where(lane < W, fock[a, p], fock[b, p])).astype(BF16)


def all_pairs(over, table, slot, fock, ready, finish):
    zero = jnp.zeros((W, W), BF16)
    lane = lax.broadcasted_iota(jnp.int32, (W, 2 * W), 1)
    halves = None
    for p in range(PAIRS + 1):
        if p < PAIRS:
            if p in CUTS:
                ready(CUTS.index(p))
            following = [two_halves(over, table, slot, fock, p, j, zero, lane) for j in range(NK // 2)]
        if p > 0:
            right = jnp.concatenate([over[p - 1, s] for s in range(NK)], 1)
            finish(p - 1, dot_t(jnp.concatenate(halves, 1), right))
        halves = following


def chunk_copy(src, dst, sem, c):
    part = pl.ds(CUTS[c], CUTS[c + 1] - CUTS[c])
    return pltpu.make_async_copy(src.at[part], dst.at[part], sem.at[c])


def row_body(first, slot, fock, sizes, shift, eps, *refs):
    pieces, refs = refs[:8], refs[8:]
    over_h, amp_h, exch_h, refs = refs[0], refs[1], refs[2], refs[3:]
    base_h, refs = refs[0], refs[1:]
    over, table, amp, exch, base, over_sem, amp_sem, exch_sem, base_sem = refs
    me = lax.axis_index("row")
    core = lax.rem(me, 2)
    def fetch(c):
        chunk_copy(over_h, over, over_sem, c).start()
        chunk_copy(amp_h, amp, amp_sem, c).start()
        chunk_copy(exch_h, exch, exch_sem, c).start()

    for c in range(AHEAD):
        fetch(c)
    eps_t = jnp.transpose(eps[...])
    for dz in range(NZ):
        chip = 8 * lax.rem(me // 2 + NZ - dz, NZ)
        for part, from_core in ((0, core), (1, 1 - core)):
            for e in range(4):
                table[chip + 4 * from_core + e] = pieces[NZ * part + dz][4 * part + e]

    def ready(c):
        if c + AHEAD < CHUNKS:
            fetch(c + AHEAD)
        chunk_copy(over_h, over, over_sem, c).wait()
        chunk_copy(amp_h, amp, amp_sem, c).wait()
        chunk_copy(exch_h, exch, exch_sem, c).wait()

    def finish(p, coupling):
        here = amp[p]
        if first:
            here = jnp.where(live(sizes[p]), here, 0.0)
        denominator = eps_t[:, p : p + 1] + eps[p : p + 1, :] - shift[p]
        base[p] = exch[p] + denominator * here - coupling
        if p + 1 in CUTS:
            chunk_copy(base, base_h, base_sem, CUTS.index(p + 1) - 1).start()

    all_pairs(over, table, slot, fock, ready, finish)
    for c in range(CHUNKS):
        chunk_copy(base, base_h, base_sem, c).wait()


def chunked(dtype=F32):
    return pltpu.VMEM((PAIRS, W, W), dtype)


FLOPS = 2 * 2 * 256 * W * W * W


def cost(times):
    return pl.CostEstimate(flops=times * FLOPS, bytes_accessed=16 * 2**20, transcendentals=0)


def row_part(first, slot, fock, sizes, shift, eps, pieces, over, amp, exch):
    return pl.pallas_call(
        functools.partial(row_body, first),
        in_specs=[SMEM] * 4 + [VMEM] + [VMEM] * 8 + [ANY] * 3,
        out_specs=ANY,
        out_shape=jax.ShapeDtypeStruct((PAIRS, W, W), F32),
        scratch_shapes=[
            pltpu.VMEM((PAIRS, NK, W, W), BF16),
            chunked(BF16),
            chunked(),
            chunked(),
            chunked(),
        ]
        + [pltpu.SemaphoreType.DMA((CHUNKS,))] * 4,
        compiler_params=pltpu.CompilerParams(vmem_limit_bytes=52 * 2**20),
        cost_estimate=cost(3),
        name="row_part",
    )(slot, fock, sizes, shift, eps, *pieces, over, amp, exch)


def col_body(first, slot, fock, sizes, shift, eps, *refs):
    if first:
        col_asked, lists, refs = refs[0], refs[1:9], refs[9:]
    over_h, table, amp_h, base_h, refs = refs[0], refs[1], refs[2], refs[3], refs[4:]
    amp_out, refs = refs[0], refs[1:]
    if first:
        out_col, out_row, refs = refs[0], refs[1:5], refs[5:]
    else:
        third_out, refs = refs[0], refs[1:]
    over, amp, base, third, over_sem, amp_sem, base_sem, amp_out_sem, third_sem, sems = refs
    def fetch(c):
        chunk_copy(over_h, over, over_sem, c).start()
        chunk_copy(amp_h, amp, amp_sem, c).start()
        chunk_copy(base_h, base, base_sem, c).start()

    for c in range(AHEAD):
        fetch(c)
    eps_t = jnp.transpose(eps[...])

    def ready(c):
        if c + AHEAD < CHUNKS:
            fetch(c + AHEAD)
        chunk_copy(over_h, over, over_sem, c).wait()
        chunk_copy(amp_h, amp, amp_sem, c).wait()
        chunk_copy(base_h, base, base_sem, c).wait()

    def finish(p, coupling):
        here = amp[p]
        alive = live(sizes[p])
        if first:
            here = jnp.where(alive, here, 0.0)
        denominator = eps_t[:, p : p + 1] + eps[p : p + 1, :] - shift[p]
        residual = jnp.where(alive, base[p] - coupling, 0.0)
        new = here - residual / denominator
        amp[p] = new
        if first:
            third[p] = new.astype(BF16)
        else:
            third[p] = residual
        if p + 1 in CUTS:
            chunk_copy(amp, amp_out, amp_out_sem, CUTS.index(p + 1) - 1).start()
            if not first:
                chunk_copy(third, third_out, third_sem, CUTS.index(p + 1) - 1).start()

    all_pairs(over, table, slot, fock, ready, finish)
    if first:
        for copy in start_outgoing(third, col_asked, lists, out_col, out_row, sems):
            copy.wait()
    for c in range(CHUNKS):
        chunk_copy(amp, amp_out, amp_out_sem, c).wait()
        if not first:
            chunk_copy(third, third_out, third_sem, c).wait()


def col_part(first, slot, fock, sizes, shift, eps, asked, over, table, amp, base):
    whole = jax.ShapeDtypeStruct((PAIRS, W, W), F32)
    return pl.pallas_call(
        functools.partial(col_body, first),
        in_specs=[SMEM] * 4 + [VMEM] + [SMEM] * len(asked) + [ANY, VMEM, ANY, ANY],
        out_specs=[ANY] * 2 + [VMEM] * NZ if first else [ANY] * 2,
        out_shape=[whole] + OUTGOING if first else [whole] * 2,
        scratch_shapes=[
            pltpu.VMEM((PAIRS, NK, W, W), BF16),
            chunked(),
            chunked(),
            chunked(BF16 if first else F32),
        ]
        + [pltpu.SemaphoreType.DMA((CHUNKS,))] * 5
        + [pltpu.SemaphoreType.DMA((PAIRS,))],
        compiler_params=pltpu.CompilerParams(vmem_limit_bytes=52 * 2**20),
        cost_estimate=cost(1),
        name="col_part",
    )(slot, fock, sizes, shift, eps, *asked, over, table, amp, base)


def swap_core(x):
    return lax.ppermute(x, "row", [(i, i ^ 1) for i in range(8)])


def shift_z(x, dz):
    return lax.ppermute(x, "row", [(i, (i + 2 * dz) % 8) for i in range(8)])


def row_exchange(bufs):
    same = [bufs[0]] + [shift_z(bufs[dz], dz) for dz in range(1, NZ)]
    return same + [swap_core(x) for x in same]


def shards(
    amp_start,
    exch_blocks,
    eps_virtual,
    pair_shift,
    pno_sizes,
    over_ik,
    over_kj,
    fock_ik,
    fock_kj,
    ik_slot,
    kj_slot,
    col_wants,
    row_wants,
):
    kj, ik = kj_slot.T, ik_slot.T
    f_ik, f_kj = fock_ik.T, fock_kj.T
    col_asked = lax.all_to_all(spread_wants(col_wants), "col", 0, 0, tiled=True)
    asked = [col_asked] + row_exchange([row_wants] * NZ)
    amp = amp_start
    out = first_outgoing(pno_sizes, asked, amp_start)
    for iteration in range(2):
        first = iteration == 0
        pieces = row_exchange(out[1:])
        table = lax.all_to_all(out[0].reshape(16, 2, W, W), "col", 0, 0, tiled=True).reshape(PAIRS, W, W)
        base = row_part(first, kj, f_ik, pno_sizes, pair_shift, eps_virtual, pieces, over_kj, amp, exch_blocks)
        amp, *out = col_part(
            first, ik, f_kj, pno_sizes, pair_shift, eps_virtual, asked if first else [], over_ik, table, amp, base
        )
    return (amp, out[0])


def solution(mesh):
    placed = (
        P(("row", "col"), None, None),
        P(("row", "col"), None, None),
        P(("row", "col"), None),
        P(("row", "col")),
        P(("row", "col")),
        P(("row", "col"), None, None, None),
        P(("row", "col"), None, None, None),
        P(("row", "col"), None),
        P(("row", "col"), None),
        P(("row", "col"), None),
        P(("row", "col"), None),
        P("row", "col", None),
        P("row", "col", None),
    )
    return jax.shard_map(
        shards,
        mesh=mesh,
        in_specs=placed,
        out_specs=(P(("row", "col"), None, None), P(("row", "col"), None, None)),
        check_vma=False,
    )
```

```python
import functools

import jax
import jax.numpy as jnp
from jax import lax
from jax.experimental import pallas as pl
from jax.experimental.pallas import tpu as pltpu
from jax.sharding import PartitionSpec as P

F32 = jnp.float32
BF16 = jnp.bfloat16
W = 128
PAIRS = 32
NK = 8
CUTS = (0, 2, 10, 18, 26, 32)
CHUNKS = len(CUTS) - 1
AHEAD = 2
NZ = 4
ANY = pl.BlockSpec(memory_space=pl.ANY)
SMEM = pl.BlockSpec(memory_space=pltpu.SMEM)
VMEM = pl.BlockSpec(memory_space=pltpu.VMEM)


def live(size):
    rows = lax.broadcasted_iota(jnp.int32, (W, W), 0) < size
    lanes = lax.broadcasted_iota(jnp.int32, (W, W), 1) < size
    return jnp.logical_and(rows, lanes)


def spread_body(wants, out):
    lane = lax.broadcasted_iota(jnp.int32, (1, W), 1)
    for q in range(out.shape[0]):
        out[q] = jnp.where(lane == 0, wants[0, 0, 2 * q], wants[0, 0, 2 * q + 1])


def spread_wants(col_wants):
    return pl.pallas_call(
        spread_body,
        in_specs=[SMEM],
        out_specs=VMEM,
        out_shape=jax.ShapeDtypeStruct((16, 1, W), jnp.int32),
        name="spread_wants",
    )(col_wants)


def start_outgoing(rounded, col_asked, lists, out_col, out_row, sems):
    copies = []
    for k in range(PAIRS):
        wanted = col_asked[k // 2, 0, k % 2]
        copies.append(pltpu.make_async_copy(rounded.at[wanted], out_col.at[k], sems.at[k]))
    for copy in copies:
        copy.start()
    me = lax.axis_index("row")
    for dz in range(NZ):
        back = (NZ - dz) % NZ
        for part in range(2):
            for e in range(4):
                out_row[dz][4 * part + e] = rounded[lists[4 * part + back][0, 0, 4 * me + e]]
    return copies


def first_body(sizes, col_asked, *refs):
    lists, amp, out_col, out_row, rounded, sems = refs[:8], refs[8], refs[9], refs[10:14], refs[14], refs[15]

    def step(p, carry):
        rounded[p] = jnp.where(live(sizes[p]), amp[p], 0.0).astype(BF16)
        return carry

    lax.fori_loop(0, PAIRS, step, 0, unroll=4)
    for copy in start_outgoing(rounded, col_asked, lists, out_col, out_row, sems):
        copy.wait()


OUTGOING = [jax.ShapeDtypeStruct((PAIRS, W, W), BF16)] + [jax.ShapeDtypeStruct((8, W, W), BF16)] * NZ


def first_outgoing(sizes, asked, amp_start):
    return pl.pallas_call(
        first_body,
        in_specs=[SMEM] + [SMEM] * 9 + [VMEM],
        out_specs=[ANY] + [VMEM] * NZ,
        out_shape=OUTGOING,
        scratch_shapes=[pltpu.VMEM((PAIRS, W, W), BF16), pltpu.SemaphoreType.DMA((PAIRS,))],
        compiler_params=pltpu.CompilerParams(vmem_limit_bytes=52 * 2**20),
        name="first_outgoing",
    )(sizes, *asked, amp_start)


def dot(a, b):
    return jnp.dot(a, b, preferred_element_type=F32)


def dot_t(a, b):
    return lax.dot_general(a, b, (((1,), (1,)), ((), ())), preferred_element_type=F32)


def two_halves(over, table, slot, fock, p, j, zero, lane):
    a, b = 2 * j, 2 * j + 1
    left = jnp.concatenate([over[p, a], over[p, b]], 1)
    blocks = jnp.concatenate(
        [
            jnp.concatenate([table[slot[a, p]], zero], 1),
            jnp.concatenate([zero, table[slot[b, p]]], 1),
        ],
        0,
    )
    return (dot(left, blocks) * jnp.where(lane < W, fock[a, p], fock[b, p])).astype(BF16)


def all_pairs(over, table, slot, fock, ready, finish):
    zero = jnp.zeros((W, W), BF16)
    lane = lax.broadcasted_iota(jnp.int32, (W, 2 * W), 1)
    halves = None
    for p in range(PAIRS + 1):
        if p < PAIRS:
            if p in CUTS:
                ready(CUTS.index(p))
            following = [two_halves(over, table, slot, fock, p, j, zero, lane) for j in range(NK // 2)]
        if p > 0:
            right = jnp.concatenate([over[p - 1, s] for s in range(NK)], 1)
            finish(p - 1, dot_t(jnp.concatenate(halves, 1), right))
        halves = following


def chunk_copy(src, dst, sem, c):
    part = pl.ds(CUTS[c], CUTS[c + 1] - CUTS[c])
    return pltpu.make_async_copy(src.at[part], dst.at[part], sem.at[c])


def row_body(first, slot, fock, sizes, shift, eps, *refs):
    pieces, refs = refs[:8], refs[8:]
    over_h, amp_h, exch_h, refs = refs[0], refs[1], refs[2], refs[3:]
    base_h, refs = refs[0], refs[1:]
    over, table, amp, exch, base, over_sem, amp_sem, exch_sem, base_sem = refs
    me = lax.axis_index("row")
    core = lax.rem(me, 2)
    def fetch(c):
        chunk_copy(over_h, over, over_sem, c).start()
        chunk_copy(amp_h, amp, amp_sem, c).start()
        chunk_copy(exch_h, exch, exch_sem, c).start()

    for c in range(AHEAD):
        fetch(c)
    eps_t = jnp.transpose(eps[...])
    for dz in range(NZ):
        chip = 8 * lax.rem(me // 2 + NZ - dz, NZ)
        for part, from_core in ((0, core), (1, 1 - core)):
            for e in range(4):
                table[chip + 4 * from_core + e] = pieces[NZ * part + dz][4 * part + e]

    def ready(c):
        if c + AHEAD < CHUNKS:
            fetch(c + AHEAD)
        chunk_copy(over_h, over, over_sem, c).wait()
        chunk_copy(amp_h, amp, amp_sem, c).wait()
        chunk_copy(exch_h, exch, exch_sem, c).wait()

    def finish(p, coupling):
        here = amp[p]
        if first:
            here = jnp.where(live(sizes[p]), here, 0.0)
        denominator = eps_t[:, p : p + 1] + eps[p : p + 1, :] - shift[p]
        base[p] = exch[p] + denominator * here - coupling
        if p + 1 in CUTS:
            chunk_copy(base, base_h, base_sem, CUTS.index(p + 1) - 1).start()

    all_pairs(over, table, slot, fock, ready, finish)
    for c in range(CHUNKS):
        chunk_copy(base, base_h, base_sem, c).wait()


def chunked(dtype=F32):
    return pltpu.VMEM((PAIRS, W, W), dtype)


FLOPS = 2 * 2 * 256 * W * W * W


def cost(times):
    return pl.CostEstimate(flops=times * FLOPS, bytes_accessed=16 * 2**20, transcendentals=0)


def row_part(first, slot, fock, sizes, shift, eps, pieces, over, amp, exch):
    return pl.pallas_call(
        functools.partial(row_body, first),
        in_specs=[SMEM] * 4 + [VMEM] + [VMEM] * 8 + [ANY] * 3,
        out_specs=ANY,
        out_shape=jax.ShapeDtypeStruct((PAIRS, W, W), F32),
        scratch_shapes=[
            pltpu.VMEM((PAIRS, NK, W, W), BF16),
            chunked(BF16),
            chunked(),
            chunked(),
            chunked(),
        ]
        + [pltpu.SemaphoreType.DMA((CHUNKS,))] * 4,
        compiler_params=pltpu.CompilerParams(vmem_limit_bytes=52 * 2**20),
        cost_estimate=cost(3),
        name="row_part",
    )(slot, fock, sizes, shift, eps, *pieces, over, amp, exch)


def col_body(first, slot, fock, sizes, shift, eps, *refs):
    if first:
        col_asked, lists, refs = refs[0], refs[1:9], refs[9:]
    over_h, table, amp_h, base_h, refs = refs[0], refs[1], refs[2], refs[3], refs[4:]
    amp_out, refs = refs[0], refs[1:]
    if first:
        out_col, out_row, refs = refs[0], refs[1:5], refs[5:]
    else:
        third_out, refs = refs[0], refs[1:]
    over, amp, base, third, over_sem, amp_sem, base_sem, amp_out_sem, third_sem, sems = refs
    def fetch(c):
        chunk_copy(over_h, over, over_sem, c).start()
        chunk_copy(amp_h, amp, amp_sem, c).start()
        chunk_copy(base_h, base, base_sem, c).start()

    for c in range(AHEAD):
        fetch(c)
    eps_t = jnp.transpose(eps[...])

    def ready(c):
        if c + AHEAD < CHUNKS:
            fetch(c + AHEAD)
        chunk_copy(over_h, over, over_sem, c).wait()
        chunk_copy(amp_h, amp, amp_sem, c).wait()
        chunk_copy(base_h, base, base_sem, c).wait()

    def finish(p, coupling):
        here = amp[p]
        alive = live(sizes[p])
        if first:
            here = jnp.where(alive, here, 0.0)
        denominator = eps_t[:, p : p + 1] + eps[p : p + 1, :] - shift[p]
        residual = jnp.where(alive, base[p] - coupling, 0.0)
        new = here - residual / denominator
        amp[p] = new
        if first:
            third[p] = new.astype(BF16)
        else:
            third[p] = residual
        if p + 1 in CUTS:
            chunk_copy(amp, amp_out, amp_out_sem, CUTS.index(p + 1) - 1).start()
            if not first:
                chunk_copy(third, third_out, third_sem, CUTS.index(p + 1) - 1).start()

    all_pairs(over, table, slot, fock, ready, finish)
    if first:
        for copy in start_outgoing(third, col_asked, lists, out_col, out_row, sems):
            copy.wait()
    for c in range(CHUNKS):
        chunk_copy(amp, amp_out, amp_out_sem, c).wait()
        if not first:
            chunk_copy(third, third_out, third_sem, c).wait()


def col_part(first, slot, fock, sizes, shift, eps, asked, over, table, amp, base):
    whole = jax.ShapeDtypeStruct((PAIRS, W, W), F32)
    return pl.pallas_call(
        functools.partial(col_body, first),
        in_specs=[SMEM] * 4 + [VMEM] + [SMEM] * len(asked) + [ANY, VMEM, ANY, ANY],
        out_specs=[ANY] * 2 + [VMEM] * NZ if first else [ANY] * 2,
        out_shape=[whole] + OUTGOING if first else [whole] * 2,
        scratch_shapes=[
            pltpu.VMEM((PAIRS, NK, W, W), BF16),
            chunked(),
            chunked(),
            chunked(BF16 if first else F32),
        ]
        + [pltpu.SemaphoreType.DMA((CHUNKS,))] * 5
        + [pltpu.SemaphoreType.DMA((PAIRS,))],
        compiler_params=pltpu.CompilerParams(vmem_limit_bytes=52 * 2**20),
        cost_estimate=cost(1),
        name="col_part",
    )(slot, fock, sizes, shift, eps, *asked, over, table, amp, base)


def swap_core(x):
    return lax.ppermute(x, "row", [(i, i ^ 1) for i in range(8)])


def shift_z(x, dz):
    return lax.ppermute(x, "row", [(i, (i + 2 * dz) % 8) for i in range(8)])


def row_exchange(bufs):
    same = [bufs[0]] + [shift_z(bufs[dz], dz) for dz in range(1, NZ)]
    return same + [swap_core(x) for x in same]


def shards(
    amp_start,
    exch_blocks,
    eps_virtual,
    pair_shift,
    pno_sizes,
    over_ik,
    over_kj,
    fock_ik,
    fock_kj,
    ik_slot,
    kj_slot,
    col_wants,
    row_wants,
):
    kj, ik = kj_slot.T, ik_slot.T
    f_ik, f_kj = fock_ik.T, fock_kj.T
    col_asked = lax.all_to_all(spread_wants(col_wants), "col", 0, 0, tiled=True)
    asked = [col_asked] + row_exchange([row_wants] * NZ)
    amp = amp_start
    out = first_outgoing(pno_sizes, asked, amp_start)
    for iteration in range(2):
        first = iteration == 0
        pieces = row_exchange(out[1:])
        table = lax.all_to_all(out[0].reshape(16, 2, W, W), "col", 0, 0, tiled=True).reshape(PAIRS, W, W)
        base = row_part(first, kj, f_ik, pno_sizes, pair_shift, eps_virtual, pieces, over_kj, amp, exch_blocks)
        amp, *out = col_part(
            first, ik, f_kj, pno_sizes, pair_shift, eps_virtual, asked if first else [], over_ik, table, amp, base
        )
    return (amp, out[0])


def solution(mesh):
    placed = (
        P(("row", "col"), None, None),
        P(("row", "col"), None, None),
        P(("row", "col"), None),
        P(("row", "col")),
        P(("row", "col")),
        P(("row", "col"), None, None, None),
        P(("row", "col"), None, None, None),
        P(("row", "col"), None),
        P(("row", "col"), None),
        P(("row", "col"), None),
        P(("row", "col"), None),
        P("row", "col", None),
        P("row", "col", None),
    )
    return jax.shard_map(
        shards,
        mesh=mesh,
        in_specs=placed,
        out_specs=(P(("row", "col"), None, None), P(("row", "col"), None, None)),
        check_vma=False,
    )
```
